512 devices in a mesh: dp: 32 (over y, x, z_hi), tensor: 16 (over z_lo, core).
Axes of the slice: x: 4, y: 4, z: 16 (z_hi: 2, z_lo: 8; z = z_hi * 8 + z_lo), core: 2. Of those that a mesh axis runs over, the one named last changes fastest.
Arguments:
- grads: bfloat16 [32, 6144, 512], P(None, ('tensor', 'dp')), may hold values from -100 to 100
- d_query: bfloat16 [4096, 6144], P('dp', 'tensor'), may hold values from -6 to 6
- w_query: bfloat16 [6144, 6144], P('dp', 'tensor'), may hold values from -0.078125 to 0.078125
Outputs:
- updates: float32 [32, 6144, 512], P(None, ('tensor', 'dp'))
- d_input: float32 [4096, 6144], P('dp', 'tensor')
The draws below stay inside these ranges and needn't reach their ends.
All inputs are finite; a program needn't handle non-finite values.
Results may differ from the reference program's by a relative error of at most 0.0005.
Values may be sent and summed in bfloat16 or wider, within the bound.
No kernel may reach another device: no remote copies, remote signals or barrier semaphores. Data moves between devices by JAX's collectives and lax.ppermute only.
A program may use at most 64 MiB of HBM per device.

```python
import math
import jax
import jax.numpy as jnp
from jax import lax

D = 6144
KV = 512
HD = 128
HEADS = 48
ITERS = 3
TOKENS = 4096
MATS = 32


def draw_grads(key, part):
    key = jax.random.fold_in(key, 11)
    key_noise, key_rows, key_cols = jax.random.split(key, 3)
    rows = jnp.exp(2.302585 * jax.random.uniform(key_rows, (MATS, D, 1), jnp.float32))
    cols = jnp.exp(2.302585 * jax.random.uniform(key_cols, (MATS, 1, KV), jnp.float32))
    position = jnp.arange(D, dtype=jnp.float32).reshape(1, D, 1) / D
    ramp = jnp.exp(0.693147 * position)
    noise = jax.random.truncated_normal(key_noise, -4.0, 4.0, (MATS, D, KV), jnp.float32)
    values = 0.1 * ramp * rows * cols * noise
    return values.astype(jnp.bfloat16)


def block_scale(own_key, shape, pieces, least, top_value):
    level = 1.0
    for dim, blocks in pieces:
        draws = jax.random.uniform(jax.random.fold_in(jax.random.fold_in(own_key, 6), dim), (blocks,), jnp.float32, least / len(pieces), top_value / len(pieces))
        level = level * jnp.repeat(jnp.exp(draws), shape[dim] // blocks).reshape((-1,) + (1,) * (len(shape) - 1 - dim))
    return level


def centred(own_key, extent, scale, bound, cuts=(), kind=jnp.bfloat16):
    array = scale * jax.random.normal(own_key, extent, jnp.float32)
    if cuts:
        array = array * block_scale(own_key, extent, cuts, -0.22, 0.18)
    return jnp.clip(array, -bound, bound).astype(kind)


def setup_inputs(seed: int = 0) -> dict:
    keys = jax.random.split(jax.random.key(seed), 4)
    grads = draw_grads(jax.random.fold_in(keys[3], 71), 0)
    d_query = centred(keys[1], (TOKENS, HEADS * HD), 1.0, 6.0, ((0, 32), (1, 16)))
    w_query = centred(keys[2], (D, HEADS * HD), D ** -0.5, 0.078125, ((0, 32), (1, 16)))
    return dict(grads=grads, d_query=d_query, w_query=w_query)


COEF_A = 3.4445
COEF_B = -4.775
COEF_C = 2.0315

def orthogonalize(block):
    wide = block.astype(jnp.float32)
    total = jnp.sum(wide * wide)
    ortho = wide / (jnp.sqrt(total) + 1e-07)
    factor = math.sqrt(block.shape[0])
    result = ortho
    for step in range(ITERS):
        gram = jnp.dot(ortho.T, ortho, preferred_element_type=jnp.float32, precision=lax.Precision.HIGHEST)
        squared = jnp.dot(gram, gram, preferred_element_type=jnp.float32, precision=lax.Precision.HIGHEST)
        poly = COEF_B * gram + COEF_C * squared
        moved = jnp.dot(ortho, poly, preferred_element_type=jnp.float32, precision=lax.Precision.HIGHEST)
        following = COEF_A * ortho + moved
        if step + 1 < ITERS:
            ortho = following
        else:
            result = factor * following
    return result

def reference(grads, d_query, w_query):
    updates = lax.map(orthogonalize, grads)
    d_input = lax.dot_general(d_query, w_query, (((1,), (1,)), ((), ())), preferred_element_type=jnp.float32)
    return (updates, d_input)
```

```python
import functools
import math

import jax
import jax.numpy as jnp
from jax import lax
from jax.experimental import pallas as pl
from jax.experimental.pallas import tpu as pltpu
from jax.sharding import Mesh, PartitionSpec as P

D = 6144
KV = 512
ITERS = 3
COEF_A = 3.4445
COEF_B = -4.775
COEF_C = 2.0315
BLK = 128
NB = KV // BLK
PAIRS = [(i, j) for i in range(NB) for j in range(i, NB)]
TINY = 2.0**-44
HALF_SCALE = 256.0

AXES = ("y", "x", "zh", "zl", "core")
COLUMN = ("zh", "zl", "core")
PLANE = ("y", "x")
F32 = jnp.float32
BF16 = jnp.bfloat16


def params(mib):
    return pltpu.CompilerParams(vmem_limit_bytes=mib << 20)


def gram_kernel(x_ref, o_ref):
    x = x_ref[...]
    gram = lax.dot_general(x, x, (((0,), (0,)), ((), ())), preferred_element_type=F32)
    for k, (i, j) in enumerate(PAIRS):
        o_ref[k * BLK : (k + 1) * BLK, :] = gram[i * BLK : (i + 1) * BLK, j * BLK : (j + 1) * BLK]


def gram_blocks(x):
    return pl.pallas_call(
        gram_kernel,
        out_shape=jax.ShapeDtypeStruct((len(PAIRS) * BLK, BLK), F32),
        compiler_params=params(16),
        cost_estimate=pl.CostEstimate(flops=2 * x.shape[0] * KV * KV, bytes_accessed=1 << 20, transcendentals=0),
        name="gram_blocks",
    )(x)


def sum_kernel(r_ref, o_ref):
    total = jnp.sum(r_ref[...], axis=0)
    for k in range(o_ref.shape[0]):
        o_ref[k] = total


def sum_and_repeat(r):
    return pl.pallas_call(
        sum_kernel,
        out_shape=jax.ShapeDtypeStruct(r.shape, F32),
        compiler_params=params(16),
        cost_estimate=pl.CostEstimate(flops=r.size, bytes_accessed=8 * r.size, transcendentals=0),
        name="sum_and_repeat",
    )(r)


def two(x):
    high = x.astype(BF16)
    return high, (x - high.astype(F32)).astype(BF16)


def mm(a, b):
    dot = functools.partial(jnp.dot, preferred_element_type=F32)
    return dot(a[0], b[0]) + (dot(a[0], b[1]) + dot(a[1], b[0]))


def newton_kernel(g_ref, x_ref, lift_ref, o_ref, m_ref):
    trace = jnp.zeros((1, 1), F32)
    for k, (i, j) in enumerate(PAIRS):
        block = g_ref[k * BLK : (k + 1) * BLK, :]
        m_ref[i * BLK : (i + 1) * BLK, j * BLK : (j + 1) * BLK] = block
        if i != j:
            m_ref[j * BLK : (j + 1) * BLK, i * BLK : (i + 1) * BLK] = block.T
        else:
            row = lax.broadcasted_iota(jnp.int32, (BLK, BLK), 0)
            col = lax.broadcasted_iota(jnp.int32, (BLK, BLK), 1)
            trace += jnp.sum(jnp.where(row == col, block, 0.0), keepdims=True)
    inverse = 1.0 / (jnp.sqrt(trace) + 1e-07)
    gram = m_ref[...] * inverse * inverse
    x = None
    for step in range(ITERS):
        parts = two(gram)
        rest = COEF_B * gram + COEF_C * mm(parts, parts)
        rest_parts = two(rest)
        if step + 1 < ITERS:
            half = COEF_A * gram + mm(parts, rest_parts)
            gram = COEF_A * half + mm(two(half), rest_parts)
        if step == 0:
            first = x_ref[...]
            dot = functools.partial(jnp.dot, preferred_element_type=F32)
            x = COEF_A * first.astype(F32) + (dot(first, rest_parts[0]) + dot(first, rest_parts[1]))
        else:
            x = COEF_A * x + mm(two(x), rest_parts)
    o_ref[...] = x * ((inverse * (math.sqrt(D) * HALF_SCALE)) * lift_ref[...])


def newton(g, x, lift):
    return pl.pallas_call(
        newton_kernel,
        out_shape=jax.ShapeDtypeStruct(x.shape, F32),
        scratch_shapes=[pltpu.VMEM((KV, KV), F32)],
        compiler_params=params(24),
        cost_estimate=pl.CostEstimate(flops=27 * 2 * KV**3, bytes_accessed=3 << 20, transcendentals=0),
        name="newton",
    )(g, x, lift)


def project_kernel(zh_ref, place_ref, q_ref, *refs):
    w_refs, (own_ref, other_ref) = refs[:-2], refs[-2:]
    zh = zh_ref[0]
    for ref, half in ((other_ref, 1 - zh), (own_ref, zh)):
        total = jnp.zeros(ref.shape, F32)
        for i, w_ref in enumerate(w_refs):
            for j in range(w_ref.shape[0]):
                q = q_ref[half, place_ref[i * w_ref.shape[0] + j]]
                total += lax.dot_general(q, w_ref[j], (((1,), (1,)), ((), ())), preferred_element_type=F32)
        ref[...] = total


def project(zh, place, q, ws):
    tokens, k = q.shape[2:]
    features = ws[0].shape[1]
    out = jax.ShapeDtypeStruct((tokens, features), F32)
    scalars = pl.BlockSpec(memory_space=pltpu.SMEM)
    return pl.pallas_call(
        project_kernel,
        in_specs=[scalars, scalars] + [pl.BlockSpec(memory_space=pltpu.VMEM)] * (1 + len(ws)),
        out_shape=[out, out],
        compiler_params=params(24),
        cost_estimate=pl.CostEstimate(flops=2 * q.size * features, bytes_accessed=6 << 20, transcendentals=0),
        name="project",
    )(zh, place, q, *ws)


def chunk_scale(rows):
    top = jnp.max(jnp.abs(rows.astype(F32)), axis=(1, 2), keepdims=True)
    return jnp.where((top < TINY) & (top > 0.0), TINY / jnp.maximum(top, 2.0**-126), 1.0)


def exchange(x, axes):
    return lax.all_to_all(x, axes, split_axis=0, concat_axis=0, tiled=True)


def round_ring(x, axis, steps):
    return [lax.ppermute(x, axis, [(i, (i + k) % 4) for i in range(4)]) for k in steps]


def turn(sizes):
    plane = sizes["y"] * sizes["x"]
    line = sizes["zl"] * sizes["core"]
    return [(p * line + t, (t ^ p) * line + p) for p in range(plane) for t in range(line)]


def body(sizes, grads, d_query, w_query):
    mats, own_rows, kv = grads.shape
    packed = (mats, own_rows * kv // BLK, BLK)
    zh = lax.axis_index("zh")
    turned = lax.ppermute(w_query, ("y", "x", "zl", "core"), turn(sizes))
    steps_y, steps_x = jnp.arange(sizes["y"])[:, None], jnp.arange(sizes["x"])[None, :]
    from_y = (lax.axis_index("y") - steps_y) % sizes["y"]
    from_x = (lax.axis_index("x") - steps_x) % sizes["x"]
    own_line = lax.axis_index(("zl", "core"))
    place = ((from_y * sizes["x"] + from_x) ^ own_line).reshape(-1).astype(jnp.int32)

    received = exchange(grads.reshape(packed), COLUMN)
    received, turned = lax.optimization_barrier((received, turned))
    rows = received.reshape(mats * own_rows, kv)
    later_query, _ = lax.optimization_barrier((d_query, received))
    queries = lax.all_gather(later_query, COLUMN, axis=0, tiled=True)
    blocks = gram_blocks(rows)
    plane = sizes["y"] * sizes["x"]
    partial, along_x = lax.optimization_barrier(
        (exchange(blocks.reshape(plane, -1, BLK), PLANE), round_ring(turned, "x", (1, 2, 3)))
    )
    along_x = jnp.stack([turned] + along_x)
    lift = jnp.repeat(chunk_scale(received).reshape(mats, 1), own_rows, axis=0)
    gram, lift = lax.optimization_barrier((exchange(sum_and_repeat(partial), PLANE).reshape(-1, BLK), lift))
    result, behind, ahead = lax.optimization_barrier((newton(gram, rows, lift), *round_ring(along_x, "y", (1, 3))))
    (opposite,) = round_ring(behind, "y", (1,))
    weights = [along_x, behind, opposite, ahead]
    sent = result.astype(jnp.float16).reshape(packed)
    returned = exchange(sent, COLUMN)

    tokens, heads = d_query.shape
    line = sizes["zl"] * sizes["core"]
    own, other = project(
        zh.reshape(1).astype(jnp.int32),
        place,
        queries.reshape(sizes["zh"], line, tokens, heads),
        weights,
    )
    returned, swapped = lax.optimization_barrier((returned, lax.ppermute(other, "zh", [(0, 1), (1, 0)])))
    updates = returned.reshape(grads.shape).astype(F32) * (1.0 / (HALF_SCALE * chunk_scale(grads)))
    first = zh == 0
    d_input = jnp.concatenate([jnp.where(first, own, swapped), jnp.where(first, swapped, own)], axis=1)
    return updates, d_input


def solution(mesh):
    sizes = dict(zip(AXES, (4, 4, 2, 8, 2)))
    fine = Mesh(mesh.devices.reshape(tuple(sizes.values())), AXES)
    rows = P(None, ("zl", "core", "y", "x", "zh"), None)
    flat = P(("y", "x", "zh"), ("zl", "core"))
    return jax.shard_map(
        functools.partial(body, sizes),
        mesh=fine,
        in_specs=(rows, flat, flat),
        out_specs=(rows, flat),
        check_vma=False,
    )
```

```python
import functools
import math

import jax
import jax.numpy as jnp
from jax import lax
from jax.experimental import pallas as pl
from jax.experimental.pallas import tpu as pltpu
from jax.sharding import Mesh, PartitionSpec as P

D = 6144
KV = 512
ITERS = 3
COEF_A = 3.4445
COEF_B = -4.775
COEF_C = 2.0315
BLK = 128
NB = KV // BLK
PAIRS = [(i, j) for i in range(NB) for j in range(i, NB)]
TINY = 2.0**-44
HALF_SCALE = 256.0

AXES = ("y", "x", "zh", "zl", "core")
COLUMN = ("zh", "zl", "core")
PLANE = ("y", "x")
F32 = jnp.float32
BF16 = jnp.bfloat16


def params(mib):
    return pltpu.CompilerParams(vmem_limit_bytes=mib << 20)


def gram_kernel(x_ref, o_ref):
    x = x_ref[...]
    gram = lax.dot_general(x, x, (((0,), (0,)), ((), ())), preferred_element_type=F32)
    for k, (i, j) in enumerate(PAIRS):
        o_ref[k * BLK : (k + 1) * BLK, :] = gram[i * BLK : (i + 1) * BLK, j * BLK : (j + 1) * BLK]


def gram_blocks(x):
    return pl.pallas_call(
        gram_kernel,
        out_shape=jax.ShapeDtypeStruct((len(PAIRS) * BLK, BLK), F32),
        compiler_params=params(16),
        cost_estimate=pl.CostEstimate(flops=2 * x.shape[0] * KV * KV, bytes_accessed=1 << 20, transcendentals=0),
        name="gram_blocks",
    )(x)


def sum_kernel(r_ref, o_ref):
    total = jnp.sum(r_ref[...], axis=0)
    for k in range(o_ref.shape[0]):
        o_ref[k] = total


def sum_and_repeat(r):
    return pl.pallas_call(
        sum_kernel,
        out_shape=jax.ShapeDtypeStruct(r.shape, F32),
        compiler_params=params(16),
        cost_estimate=pl.CostEstimate(flops=5 * 10**9, bytes_accessed=8 * r.size, transcendentals=0),
        name="sum_and_repeat",
    )(r)


def relay_kernel(x_ref, o_ref):
    o_ref[...] = x_ref[...]


def relay(x):
    return pl.pallas_call(
        relay_kernel,
        out_shape=jax.ShapeDtypeStruct(x.shape, x.dtype),
        compiler_params=params(16),
        cost_estimate=pl.CostEstimate(flops=5 * 10**10, bytes_accessed=4 * x.size, transcendentals=0),
        name="relay",
    )(x)


def two(x):
    high = x.astype(BF16)
    return high, (x - high.astype(F32)).astype(BF16)


def mm(a, b):
    dot = functools.partial(jnp.dot, preferred_element_type=F32)
    return dot(a[0], b[0]) + (dot(a[0], b[1]) + dot(a[1], b[0]))


def newton_kernel(g_ref, x_ref, lift_ref, o_ref, m_ref):
    trace = jnp.zeros((1, 1), F32)
    for k, (i, j) in enumerate(PAIRS):
        block = g_ref[k * BLK : (k + 1) * BLK, :]
        m_ref[i * BLK : (i + 1) * BLK, j * BLK : (j + 1) * BLK] = block
        if i != j:
            m_ref[j * BLK : (j + 1) * BLK, i * BLK : (i + 1) * BLK] = block.T
        else:
            row = lax.broadcasted_iota(jnp.int32, (BLK, BLK), 0)
            col = lax.broadcasted_iota(jnp.int32, (BLK, BLK), 1)
            trace += jnp.sum(jnp.where(row == col, block, 0.0), keepdims=True)
    inverse = 1.0 / (jnp.sqrt(trace) + 1e-07)
    gram = m_ref[...] * inverse * inverse
    x = None
    for step in range(ITERS):
        parts = two(gram)
        rest = COEF_B * gram + COEF_C * mm(parts, parts)
        rest_parts = two(rest)
        if step + 1 < ITERS:
            half = COEF_A * gram + mm(parts, rest_parts)
            gram = COEF_A * half + mm(two(half), rest_parts)
        if step == 0:
            first = x_ref[...]
            dot = functools.partial(jnp.dot, preferred_element_type=F32)
            x = COEF_A * first.astype(F32) + (dot(first, rest_parts[0]) + dot(first, rest_parts[1]))
        else:
            x = COEF_A * x + mm(two(x), rest_parts)
    o_ref[...] = x * ((inverse * (math.sqrt(D) * HALF_SCALE)) * lift_ref[...])


def newton(g, x, lift):
    return pl.pallas_call(
        newton_kernel,
        out_shape=jax.ShapeDtypeStruct(x.shape, F32),
        scratch_shapes=[pltpu.VMEM((KV, KV), F32)],
        compiler_params=params(24),
        cost_estimate=pl.CostEstimate(flops=27 * 2 * KV**3, bytes_accessed=3 << 20, transcendentals=0),
        name="newton",
    )(g, x, lift)


def project_kernel(zh_ref, place_ref, q_ref, *refs):
    w_refs, (own_ref, other_ref) = refs[:-2], refs[-2:]
    zh = zh_ref[0]
    for ref, half in ((other_ref, 1 - zh), (own_ref, zh)):
        total = jnp.zeros(ref.shape, F32)
        for i, w_ref in enumerate(w_refs):
            for j in range(w_ref.shape[0]):
                q = q_ref[half, place_ref[i * w_ref.shape[0] + j]]
                total += lax.dot_general(q, w_ref[j], (((1,), (1,)), ((), ())), preferred_element_type=F32)
        ref[...] = total


def project(zh, place, q, ws):
    tokens, k = q.shape[2:]
    features = ws[0].shape[1]
    out = jax.ShapeDtypeStruct((tokens, features), F32)
    scalars = pl.BlockSpec(memory_space=pltpu.SMEM)
    return pl.pallas_call(
        project_kernel,
        in_specs=[scalars, scalars] + [pl.BlockSpec(memory_space=pltpu.VMEM)] * (1 + len(ws)),
        out_shape=[out, out],
        compiler_params=params(24),
        cost_estimate=pl.CostEstimate(flops=10**12, bytes_accessed=6 << 20, transcendentals=0),
        name="project",
    )(zh, place, q, *ws)


def chunk_scale(rows):
    top = jnp.max(jnp.abs(rows.astype(F32)), axis=(1, 2), keepdims=True)
    return jnp.where((top < TINY) & (top > 0.0), TINY / jnp.maximum(top, 2.0**-126), 1.0)


def exchange(x, axes):
    return lax.all_to_all(x, axes, split_axis=0, concat_axis=0, tiled=True)


def round_ring(x, axis, steps):
    return [lax.ppermute(x, axis, [(i, (i + k) % 4) for i in range(4)]) for k in steps]


def spread(p):
    return ((p << 1) & 15) ^ ((p >> 3) * 3)


def turn(sizes):
    plane = sizes["y"] * sizes["x"]
    line = sizes["zl"] * sizes["core"]
    return [(p * line + t, (t ^ spread(p)) * line + p) for p in range(plane) for t in range(line)]


def body(sizes, grads, d_query, w_query):
    mats, own_rows, kv = grads.shape
    packed = (mats, own_rows * kv // BLK, BLK)
    zh = lax.axis_index("zh")
    turned = lax.ppermute(w_query, ("y", "x", "zl", "core"), turn(sizes))
    steps_y, steps_x = jnp.arange(sizes["y"])[:, None], jnp.arange(sizes["x"])[None, :]
    from_y = (lax.axis_index("y") - steps_y) % sizes["y"]
    from_x = (lax.axis_index("x") - steps_x) % sizes["x"]
    own_line = lax.axis_index(("zl", "core"))
    place = ((from_y * sizes["x"] + from_x) ^ spread(own_line)).reshape(-1).astype(jnp.int32)

    turned = relay(turned)
    received, along_x = lax.optimization_barrier(
        (exchange(grads.reshape(packed), COLUMN), round_ring(turned, "x", (1, 2, 3)))
    )
    along_x = jnp.stack([turned] + along_x)
    rows = received.reshape(mats * own_rows, kv)
    later_query, _ = lax.optimization_barrier((d_query, w_query))
    queries = lax.all_gather(later_query, COLUMN, axis=0, tiled=True)
    blocks = gram_blocks(rows)
    plane = sizes["y"] * sizes["x"]
    partial = exchange(blocks.reshape(plane, -1, BLK), PLANE)
    lift = jnp.repeat(chunk_scale(received).reshape(mats, 1), own_rows, axis=0)
    gram, behind, ahead, lift = lax.optimization_barrier(
        (exchange(sum_and_repeat(partial), PLANE).reshape(-1, BLK), *round_ring(along_x, "y", (1, 3)), lift)
    )
    result = newton(gram, rows, lift)
    (opposite,) = round_ring(behind, "y", (1,))
    weights = [along_x, behind, opposite, ahead]
    sent = result.astype(jnp.float16).reshape(packed)
    returned = exchange(sent, COLUMN)

    tokens, heads = d_query.shape
    line = sizes["zl"] * sizes["core"]
    own, other = project(
        zh.reshape(1).astype(jnp.int32),
        place,
        queries.reshape(sizes["zh"], line, tokens, heads),
        weights,
    )
    returned, swapped = lax.optimization_barrier((returned, lax.ppermute(other, "zh", [(0, 1), (1, 0)])))
    updates = returned.reshape(grads.shape).astype(F32) * (1.0 / (HALF_SCALE * chunk_scale(grads)))
    first = zh == 0
    d_input = jnp.concatenate([jnp.where(first, own, swapped), jnp.where(first, swapped, own)], axis=1)
    return updates, d_input


def solution(mesh):
    sizes = dict(zip(AXES, (4, 4, 2, 8, 2)))
    fine = Mesh(mesh.devices.reshape(tuple(sizes.values())), AXES)
    rows = P(None, ("zl", "core", "y", "x", "zh"), None)
    flat = P(("y", "x", "zh"), ("zl", "core"))
    return jax.shard_map(
        functools.partial(body, sizes),
        mesh=fine,
        in_specs=(rows, flat, flat),
        out_specs=(rows, flat),
        check_vma=False,
    )
```

```python
import functools
import math

import jax
import jax.numpy as jnp
from jax import lax
from jax.experimental import pallas as pl
from jax.experimental.pallas import tpu as pltpu
from jax.sharding import Mesh, PartitionSpec as P

D = 6144
KV = 512
ITERS = 3
COEF_A = 3.4445
COEF_B = -4.775
COEF_C = 2.0315
BLK = 128
NB = KV // BLK
PAIRS = [(i, j) for i in range(NB) for j in range(i, NB)]
TINY = 2.0**-44
HALF_SCALE = 256.0

AXES = ("y", "x", "zh", "zl", "core")
COLUMN = ("zh", "zl", "core")
PLANE = ("y", "x")
F32 = jnp.float32
BF16 = jnp.bfloat16


def params(mib):
    return pltpu.CompilerParams(vmem_limit_bytes=mib << 20)


def gram_kernel(x_ref, o_ref):
    x = x_ref[...]
    gram = lax.dot_general(x, x, (((0,), (0,)), ((), ())), preferred_element_type=F32)
    for k, (i, j) in enumerate(PAIRS):
        o_ref[k * BLK : (k + 1) * BLK, :] = gram[i * BLK : (i + 1) * BLK, j * BLK : (j + 1) * BLK]


def gram_blocks(x):
    return pl.pallas_call(
        gram_kernel,
        out_shape=jax.ShapeDtypeStruct((len(PAIRS) * BLK, BLK), F32),
        compiler_params=params(16),
        cost_estimate=pl.CostEstimate(flops=2 * x.shape[0] * KV * KV, bytes_accessed=1 << 20, transcendentals=0),
        name="gram_blocks",
    )(x)


def sum_kernel(r_ref, o_ref):
    total = jnp.sum(r_ref[...], axis=0)
    for k in range(o_ref.shape[0]):
        o_ref[k] = total


def sum_and_repeat(r):
    return pl.pallas_call(
        sum_kernel,
        out_shape=jax.ShapeDtypeStruct(r.shape, F32),
        compiler_params=params(16),
        cost_estimate=pl.CostEstimate(flops=5 * 10**9, bytes_accessed=8 * r.size, transcendentals=0),
        name="sum_and_repeat",
    )(r)


def relay_kernel(x_ref, o_ref):
    o_ref[...] = x_ref[...]


def relay(x):
    return pl.pallas_call(
        relay_kernel,
        out_shape=jax.ShapeDtypeStruct(x.shape, x.dtype),
        compiler_params=params(16),
        cost_estimate=pl.CostEstimate(flops=5 * 10**10, bytes_accessed=4 * x.size, transcendentals=0),
        name="relay",
    )(x)


def two(x):
    high = x.astype(BF16)
    return high, (x - high.astype(F32)).astype(BF16)


def mm(a, b):
    dot = functools.partial(jnp.dot, preferred_element_type=F32)
    return dot(a[0], b[0]) + (dot(a[0], b[1]) + dot(a[1], b[0]))


def newton_kernel(g_ref, x_ref, lift_ref, o_ref, m_ref):
    trace = jnp.zeros((1, 1), F32)
    for k, (i, j) in enumerate(PAIRS):
        block = g_ref[k * BLK : (k + 1) * BLK, :]
        m_ref[i * BLK : (i + 1) * BLK, j * BLK : (j + 1) * BLK] = block
        if i != j:
            m_ref[j * BLK : (j + 1) * BLK, i * BLK : (i + 1) * BLK] = block.T
        else:
            row = lax.broadcasted_iota(jnp.int32, (BLK, BLK), 0)
            col = lax.broadcasted_iota(jnp.int32, (BLK, BLK), 1)
            trace += jnp.sum(jnp.where(row == col, block, 0.0), keepdims=True)
    inverse = 1.0 / (jnp.sqrt(trace) + 1e-07)
    gram = m_ref[...] * inverse * inverse
    x = None
    for step in range(ITERS):
        parts = two(gram)
        rest = COEF_B * gram + COEF_C * mm(parts, parts)
        rest_parts = two(rest)
        if step + 1 < ITERS:
            half = COEF_A * gram + mm(parts, rest_parts)
            gram = COEF_A * half + mm(two(half), rest_parts)
        if step == 0:
            first = x_ref[...]
            dot = functools.partial(jnp.dot, preferred_element_type=F32)
            x = COEF_A * first.astype(F32) + (dot(first, rest_parts[0]) + dot(first, rest_parts[1]))
        else:
            x = COEF_A * x + mm(two(x), rest_parts)
    o_ref[...] = x * ((inverse * (math.sqrt(D) * HALF_SCALE)) * lift_ref[...])


def newton(g, x, lift):
    return pl.pallas_call(
        newton_kernel,
        out_shape=jax.ShapeDtypeStruct(x.shape, F32),
        scratch_shapes=[pltpu.VMEM((KV, KV), F32)],
        compiler_params=params(24),
        cost_estimate=pl.CostEstimate(flops=27 * 2 * KV**3, bytes_accessed=3 << 20, transcendentals=0),
        name="newton",
    )(g, x, lift)


def project_kernel(zh_ref, place_ref, q_ref, *refs):
    w_refs, (own_ref, other_ref) = refs[:-2], refs[-2:]
    zh = zh_ref[0]
    for ref, half in ((other_ref, 1 - zh), (own_ref, zh)):
        total = jnp.zeros(ref.shape, F32)
        for i, w_ref in enumerate(w_refs):
            for j in range(w_ref.shape[0]):
                q = q_ref[half, place_ref[i * w_ref.shape[0] + j]]
                total += lax.dot_general(q, w_ref[j], (((1,), (1,)), ((), ())), preferred_element_type=F32)
        ref[...] = total


def project(zh, place, q, ws):
    tokens, k = q.shape[2:]
    features = ws[0].shape[1]
    out = jax.ShapeDtypeStruct((tokens, features), F32)
    scalars = pl.BlockSpec(memory_space=pltpu.SMEM)
    return pl.pallas_call(
        project_kernel,
        in_specs=[scalars, scalars] + [pl.BlockSpec(memory_space=pltpu.VMEM)] * (1 + len(ws)),
        out_shape=[out, out],
        compiler_params=params(24),
        cost_estimate=pl.CostEstimate(flops=10**12, bytes_accessed=6 << 20, transcendentals=0),
        name="project",
    )(zh, place, q, *ws)


def unpack_kernel(scale_ref, x_ref, o_ref):
    mats, rows, columns = o_ref.shape
    for m in range(mats):
        x = x_ref[m] * scale_ref[m]
        for c in range(columns // BLK):
            o_ref[m, :, c * BLK : (c + 1) * BLK] = x[c * rows : (c + 1) * rows]


def unpack(scale, x, shape):
    return pl.pallas_call(
        unpack_kernel,
        in_specs=[pl.BlockSpec(memory_space=pltpu.SMEM), pl.BlockSpec(memory_space=pltpu.VMEM)],
        out_shape=jax.ShapeDtypeStruct(shape, F32),
        compiler_params=params(16),
        cost_estimate=pl.CostEstimate(flops=1, bytes_accessed=1, transcendentals=0),
        name="unpack",
    )(scale, x)


def chunk_scale(rows):
    top = jnp.max(jnp.abs(rows.astype(F32)), axis=(1, 2), keepdims=True)
    return jnp.where((top < TINY) & (top > 0.0), TINY / jnp.maximum(top, 2.0**-126), 1.0)


def exchange(x, axes):
    return lax.all_to_all(x, axes, split_axis=0, concat_axis=0, tiled=True)


def round_ring(x, axis, steps):
    return [lax.ppermute(x, axis, [(i, (i + k) % 4) for i in range(4)]) for k in steps]


def spread(p):
    return ((p << 1) & 15) ^ ((p >> 3) * 3)


def turn(sizes):
    plane = sizes["y"] * sizes["x"]
    line = sizes["zl"] * sizes["core"]
    return [(p * line + t, (t ^ spread(p)) * line + p) for p in range(plane) for t in range(line)]


def body(sizes, grads, d_query, w_query):
    mats, own_rows, kv = grads.shape
    packed = (mats, own_rows * kv // BLK, BLK)
    zh = lax.axis_index("zh")
    turned = lax.ppermute(w_query, ("y", "x", "zl", "core"), turn(sizes))
    steps_y, steps_x = jnp.arange(sizes["y"])[:, None], jnp.arange(sizes["x"])[None, :]
    from_y = (lax.axis_index("y") - steps_y) % sizes["y"]
    from_x = (lax.axis_index("x") - steps_x) % sizes["x"]
    own_line = lax.axis_index(("zl", "core"))
    place = ((from_y * sizes["x"] + from_x) ^ spread(own_line)).reshape(-1).astype(jnp.int32)

    turned = relay(turned)
    received, along_x = lax.optimization_barrier(
        (exchange(grads.reshape(packed), COLUMN), round_ring(turned, "x", (1, 2, 3)))
    )
    along_x = jnp.stack([turned] + along_x)
    rows = received.reshape(mats * own_rows, kv)
    later_query, _ = lax.optimization_barrier((d_query, w_query))
    queries = lax.all_gather(later_query, COLUMN, axis=0, tiled=True)
    blocks = gram_blocks(rows)
    plane = sizes["y"] * sizes["x"]
    partial = exchange(blocks.reshape(plane, -1, BLK), PLANE)
    lift = jnp.repeat(chunk_scale(received).reshape(mats, 1), own_rows, axis=0)
    gram, behind, ahead, lift = lax.optimization_barrier(
        (exchange(sum_and_repeat(partial), PLANE).reshape(-1, BLK), *round_ring(along_x, "y", (1, 3)), lift)
    )
    result = newton(gram, rows, lift)
    (opposite,) = round_ring(behind, "y", (1,))
    weights = [along_x, behind, opposite, ahead]
    sent = result.astype(jnp.float16).reshape(mats, own_rows, kv // BLK, BLK).transpose(0, 2, 1, 3).reshape(packed)
    returned = exchange(sent, COLUMN)

    tokens, heads = d_query.shape
    line = sizes["zl"] * sizes["core"]
    own, other = project(
        zh.reshape(1).astype(jnp.int32),
        place,
        queries.reshape(sizes["zh"], line, tokens, heads),
        weights,
    )
    swapped = lax.ppermute(other, "zh", [(0, 1), (1, 0)])
    returned, own = lax.optimization_barrier((returned, own))
    updates = unpack((1.0 / (HALF_SCALE * chunk_scale(grads))).reshape(mats), returned.astype(F32), grads.shape)
    first = zh == 0
    d_input = jnp.concatenate([jnp.where(first, own, swapped), jnp.where(first, swapped, own)], axis=1)
    return updates, d_input


def solution(mesh):
    sizes = dict(zip(AXES, (4, 4, 2, 8, 2)))
    fine = Mesh(mesh.devices.reshape(tuple(sizes.values())), AXES)
    rows = P(None, ("zl", "core", "y", "x", "zh"), None)
    flat = P(("y", "x", "zh"), ("zl", "core"))
    return jax.shard_map(
        functools.partial(body, sizes),
        mesh=fine,
        in_specs=(rows, flat, flat),
        out_specs=(rows, flat),
        check_vma=False,
    )
```

```python
import functools
import math

import jax
import jax.numpy as jnp
from jax import lax
from jax.experimental import pallas as pl
from jax.experimental.pallas import tpu as pltpu
from jax.sharding import Mesh, PartitionSpec as P

D = 6144
KV = 512
ITERS = 3
COEF_A = 3.4445
COEF_B = -4.775
COEF_C = 2.0315
BLK = 128
NB = KV // BLK
PAIRS = [(i, j) for i in range(NB) for j in range(i, NB)]
TINY = 2.0**-44
HALF_SCALE = 256.0

AXES = ("y", "x", "zh", "zl", "core")
COLUMN = ("zh", "zl", "core")
PLANE = ("y", "x")
F32 = jnp.float32
BF16 = jnp.bfloat16


def params(mib):
    return pltpu.CompilerParams(vmem_limit_bytes=mib << 20)


def gram_kernel(x_ref, o_ref):
    x = x_ref[...]
    gram = lax.dot_general(x, x, (((0,), (0,)), ((), ())), preferred_element_type=F32)
    for k, (i, j) in enumerate(PAIRS):
        o_ref[k * BLK : (k + 1) * BLK, :] = gram[i * BLK : (i + 1) * BLK, j * BLK : (j + 1) * BLK]


def gram_blocks(x):
    return pl.pallas_call(
        gram_kernel,
        out_shape=jax.ShapeDtypeStruct((len(PAIRS) * BLK, BLK), F32),
        compiler_params=params(16),
        cost_estimate=pl.CostEstimate(flops=2 * x.shape[0] * KV * KV, bytes_accessed=1 << 20, transcendentals=0),
        name="gram_blocks",
    )(x)


def sum_kernel(r_ref, o_ref):
    total = jnp.sum(r_ref[...], axis=0)
    for k in range(o_ref.shape[0]):
        o_ref[k] = total


def sum_and_repeat(r):
    return pl.pallas_call(
        sum_kernel,
        out_shape=jax.ShapeDtypeStruct(r.shape, F32),
        compiler_params=params(16),
        cost_estimate=pl.CostEstimate(flops=5 * 10**9, bytes_accessed=8 * r.size, transcendentals=0),
        name="sum_and_repeat",
    )(r)


def relay_kernel(x_ref, o_ref):
    o_ref[...] = x_ref[...]


def relay(x):
    return pl.pallas_call(
        relay_kernel,
        out_shape=jax.ShapeDtypeStruct(x.shape, x.dtype),
        compiler_params=params(16),
        cost_estimate=pl.CostEstimate(flops=5 * 10**10, bytes_accessed=4 * x.size, transcendentals=0),
        name="relay",
    )(x)


def two(x):
    high = x.astype(BF16)
    return high, (x - high.astype(F32)).astype(BF16)


def half_exponent(x):
    top = jnp.max(jnp.abs(x), keepdims=True)
    return jnp.clip(jnp.round(13.0 - jnp.log2(jnp.maximum(top, 2.0**-120))), -20.0, 120.0)


def mm(a, b):
    dot = functools.partial(jnp.dot, preferred_element_type=F32)
    return dot(a[0], b[0]) + (dot(a[0], b[1]) + dot(a[1], b[0]))


def newton_kernel(g_ref, x_ref, lift_ref, o_ref, m_ref):
    trace = jnp.zeros((1, 1), F32)
    for k, (i, j) in enumerate(PAIRS):
        block = g_ref[k * BLK : (k + 1) * BLK, :]
        m_ref[i * BLK : (i + 1) * BLK, j * BLK : (j + 1) * BLK] = block
        if i != j:
            m_ref[j * BLK : (j + 1) * BLK, i * BLK : (i + 1) * BLK] = block.T
        else:
            row = lax.broadcasted_iota(jnp.int32, (BLK, BLK), 0)
            col = lax.broadcasted_iota(jnp.int32, (BLK, BLK), 1)
            trace += jnp.sum(jnp.where(row == col, block, 0.0), keepdims=True)
    inverse = 1.0 / (jnp.sqrt(trace) + 1e-07)
    gram = m_ref[...] * inverse * inverse
    x = None
    for step in range(ITERS):
        parts = two(gram)
        rest = COEF_B * gram + COEF_C * mm(parts, parts)
        rest_parts = two(rest)
        if step + 1 < ITERS:
            half = COEF_A * gram + mm(parts, rest_parts)
            gram = COEF_A * half + mm(two(half), rest_parts)
        if step == 0:
            first = x_ref[...]
            dot = functools.partial(jnp.dot, preferred_element_type=F32)
            x = COEF_A * first.astype(F32) + (dot(first, rest_parts[0]) + dot(first, rest_parts[1]))
        else:
            x = COEF_A * x + mm(two(x), rest_parts)
    o_ref[...] = x * ((inverse * (math.sqrt(D) * HALF_SCALE)) * lift_ref[...])


def newton(g, x, lift):
    return pl.pallas_call(
        newton_kernel,
        out_shape=jax.ShapeDtypeStruct(x.shape, F32),
        scratch_shapes=[pltpu.VMEM((KV, KV), F32)],
        compiler_params=params(24),
        cost_estimate=pl.CostEstimate(flops=27 * 2 * KV**3, bytes_accessed=3 << 20, transcendentals=0),
        name="newton",
    )(g, x, lift)


def project_kernel(zh_ref, place_ref, q_ref, *refs):
    w_refs, (own_ref, other_ref) = refs[:-2], refs[-2:]
    zh = zh_ref[0]
    for ref, half in ((other_ref, 1 - zh), (own_ref, zh)):
        total = jnp.zeros(own_ref.shape, F32)
        for i, w_ref in enumerate(w_refs):
            for j in range(w_ref.shape[0]):
                q = q_ref[half, place_ref[i * w_ref.shape[0] + j]]
                total += lax.dot_general(q, w_ref[j], (((1,), (1,)), ((), ())), preferred_element_type=F32)
        if ref is own_ref:
            ref[...] = total
        else:
            exponent = half_exponent(total)
            tokens = total.shape[0]
            ref[:tokens] = total * jnp.exp2(exponent)
            ref[tokens:] = jnp.broadcast_to(exponent, (ref.shape[0] - tokens, ref.shape[1]))


def project(zh, place, q, ws):
    tokens, k = q.shape[2:]
    features = ws[0].shape[1]
    out = jax.ShapeDtypeStruct((tokens, features), F32)
    scalars = pl.BlockSpec(memory_space=pltpu.SMEM)
    return pl.pallas_call(
        project_kernel,
        in_specs=[scalars, scalars] + [pl.BlockSpec(memory_space=pltpu.VMEM)] * (1 + len(ws)),
        out_shape=[out, jax.ShapeDtypeStruct((tokens + 16, features), F32)],
        compiler_params=params(24),
        cost_estimate=pl.CostEstimate(flops=10**12, bytes_accessed=6 << 20, transcendentals=0),
        name="project",
    )(zh, place, q, *ws)


def unpack_kernel(scale_ref, x_ref, o_ref):
    mats, rows, columns = o_ref.shape
    for m in range(mats):
        x = x_ref[m] * scale_ref[m]
        for c in range(columns // BLK):
            o_ref[m, :, c * BLK : (c + 1) * BLK] = x[c * rows : (c + 1) * rows]


def unpack(scale, x, shape):
    return pl.pallas_call(
        unpack_kernel,
        in_specs=[pl.BlockSpec(memory_space=pltpu.SMEM), pl.BlockSpec(memory_space=pltpu.VMEM)],
        out_shape=jax.ShapeDtypeStruct(shape, F32),
        compiler_params=params(16),
        cost_estimate=pl.CostEstimate(flops=1, bytes_accessed=1, transcendentals=0),
        name="unpack",
    )(scale, x)


def chunk_scale(rows):
    top = jnp.max(jnp.abs(rows.astype(F32)), axis=(1, 2), keepdims=True)
    return jnp.where((top < TINY) & (top > 0.0), TINY / jnp.maximum(top, 2.0**-126), 1.0)


def exchange(x, axes):
    return lax.all_to_all(x, axes, split_axis=0, concat_axis=0, tiled=True)


def round_ring(x, axis, steps):
    return [lax.ppermute(x, axis, [(i, (i + k) % 4) for i in range(4)]) for k in steps]


def spread(p):
    return ((p << 1) & 15) ^ ((p >> 3) * 3)


def turn(sizes):
    plane = sizes["y"] * sizes["x"]
    line = sizes["zl"] * sizes["core"]
    return [(p * line + t, (t ^ spread(p)) * line + p) for p in range(plane) for t in range(line)]


def body(sizes, grads, d_query, w_query):
    mats, own_rows, kv = grads.shape
    packed = (mats, own_rows * kv // BLK, BLK)
    zh = lax.axis_index("zh")
    turned = lax.ppermute(w_query, ("y", "x", "zl", "core"), turn(sizes))
    steps_y, steps_x = jnp.arange(sizes["y"])[:, None], jnp.arange(sizes["x"])[None, :]
    from_y = (lax.axis_index("y") - steps_y) % sizes["y"]
    from_x = (lax.axis_index("x") - steps_x) % sizes["x"]
    own_line = lax.axis_index(("zl", "core"))
    place = ((from_y * sizes["x"] + from_x) ^ spread(own_line)).reshape(-1).astype(jnp.int32)

    turned = relay(turned)
    received, along_x = lax.optimization_barrier(
        (exchange(grads.reshape(packed), COLUMN), round_ring(turned, "x", (1, 2, 3)))
    )
    along_x = jnp.stack([turned] + along_x)
    rows = received.reshape(mats * own_rows, kv)
    later_query, _ = lax.optimization_barrier((d_query, w_query))
    queries = lax.all_gather(later_query, COLUMN, axis=0, tiled=True)
    blocks = gram_blocks(rows)
    plane = sizes["y"] * sizes["x"]
    partial = exchange(blocks.reshape(plane, -1, BLK), PLANE)
    lift = jnp.repeat(chunk_scale(received).reshape(mats, 1), own_rows, axis=0)
    gram, behind, ahead, lift = lax.optimization_barrier(
        (exchange(sum_and_repeat(partial), PLANE).reshape(-1, BLK), *round_ring(along_x, "y", (1, 3)), lift)
    )
    result = newton(gram, rows, lift)
    (opposite,) = round_ring(behind, "y", (1,))
    weights = [along_x, behind, opposite, ahead]
    sent = result.astype(jnp.float16).reshape(mats, own_rows, kv // BLK, BLK).transpose(0, 2, 1, 3).reshape(packed)
    returned = exchange(sent, COLUMN)

    tokens, heads = d_query.shape
    line = sizes["zl"] * sizes["core"]
    own, other = project(
        zh.reshape(1).astype(jnp.int32),
        place,
        queries.reshape(sizes["zh"], line, tokens, heads),
        weights,
    )
    swapped = lax.ppermute(other.astype(jnp.float16), "zh", [(0, 1), (1, 0)]).astype(F32)
    swapped = swapped[:-16] * jnp.exp2(-swapped[-1:, :1])
    returned, own = lax.optimization_barrier((returned, own))
    updates = unpack((1.0 / (HALF_SCALE * chunk_scale(grads))).reshape(mats), returned.astype(F32), grads.shape)
    first = zh == 0
    d_input = jnp.concatenate([jnp.where(first, own, swapped), jnp.where(first, swapped, own)], axis=1)
    return updates, d_input


def solution(mesh):
    sizes = dict(zip(AXES, (4, 4, 2, 8, 2)))
    fine = Mesh(mesh.devices.reshape(tuple(sizes.values())), AXES)
    rows = P(None, ("zl", "core", "y", "x", "zh"), None)
    flat = P(("y", "x", "zh"), ("zl", "core"))
    return jax.shard_map(
        functools.partial(body, sizes),
        mesh=fine,
        in_specs=(rows, flat, flat),
        out_specs=(rows, flat),
        check_vma=False,
    )
```
